128 devices in a mesh: gx: 16 (over x, y), gy: 4 (over z), gz: 2 (over core).
Axes of the slice: x: 4, y: 4, z: 4, core: 2. Of those that a mesh axis runs over, the one named last changes fastest.
Arguments:
- thermal_state: float32 [512, 512, 256], P('gx', 'gy', 'gz'), may hold values from -12 to 12
- material_kinds: int32 [512, 512, 256], P('gx', 'gy', 'gz'), may hold values from 0 to 7
- axial_diffusivity_by_kind: float32 [8], replicated, may hold values from 1000 to 8000
- crosswise_diffusivity_by_kind: float32 [2, 8], replicated, may hold values from 0.04 to 0.2
Outputs:
- new_temperature: float32 [512, 512, 256], P('gx', 'gy', 'gz')
The draws below stay inside these ranges and needn't reach their ends.
Inputs may be any that keep to these rules, and one draw needn't show every extreme that they name: `material_kinds`: indexes the tables' last dimension.
All inputs are finite; a program needn't handle non-finite values.
Results may differ from the reference program's by a relative error of at most 0.0003.
Values sent between devices are 32-bit elements; how exact they have to be, the bound alone decides.
No kernel may reach another device: no remote copies, remote signals or barrier semaphores. Data moves between devices by JAX's collectives and lax.ppermute only.
A program may use at most 128 MiB of HBM per device.

```python
import math
import jax
import jax.numpy as jnp
from jax import lax

NCLASS = 8
NX = 512
NY = 512
NZ = 256


def draw_thermal_state(key, part):
    key = jax.random.fold_in(key, 11)
    return 3.0 * jax.random.truncated_normal(key, -4.0, 4.0, (NX, NY, NZ), jnp.float32)


def touch_ends(values, rng, smallest, largest):
    place = [jax.random.randint(jax.random.fold_in(rng, axis), (), 0, length) for axis, length in enumerate(values.shape)]
    main_axis = values.shape.index(max(values.shape))
    beside = place[:main_axis] + [(place[main_axis] + 1) % values.shape[main_axis]] + place[main_axis + 1:]
    return values.at[tuple(place)].set(smallest).at[tuple(beside)].set(largest)


def setup_inputs(seed: int = 0) -> dict:
    key_list = jax.random.split(jax.random.key(seed), 5)
    return {
        "thermal_state": draw_thermal_state(jax.random.fold_in(key_list[4], 71), 0),
        "material_kinds": touch_ends(jax.random.randint(key_list[1], (NX, NY, NZ), 0, NCLASS), jax.random.fold_in(key_list[1], 1), 0, NCLASS - 1).astype(jnp.int32),
        "axial_diffusivity_by_kind": jnp.clip(jnp.exp(jax.random.uniform(key_list[2], (NCLASS,), jnp.float32, math.log(1000.0), math.log(8000.0))), 1000.0, 8000.0),
        "crosswise_diffusivity_by_kind": jnp.clip(jnp.exp(jax.random.uniform(key_list[3], (2, NCLASS), jnp.float32, math.log(0.04), math.log(0.2))), 0.04, 0.2),
    }


def solve_lines(lower_band, main_band, upper_band, thermal_forcing_rhs):
    def forward(running, row_data):
        ratio_before, value_before = running
        lower_row, main_row, upper_row, source_row = row_data
        divisor = main_row - lower_row * ratio_before
        ratio_now = upper_row / divisor
        value_now = (source_row - lower_row[None] * value_before) / divisor[None]
        return (ratio_now, value_now), (ratio_now, value_now)

    start = (jnp.zeros_like(main_band[0]), jnp.zeros_like(thermal_forcing_rhs[0]))
    _, (ratios, values) = lax.scan(forward, start, (lower_band, main_band, upper_band, thermal_forcing_rhs))

    def backward(following, row_data):
        ratio_row, value_row = row_data
        solved = value_row - ratio_row[None] * following
        return solved, solved

    _, result = lax.scan(backward, jnp.zeros_like(thermal_forcing_rhs[0]), (ratios, values), reverse=True)
    return result


def reference(thermal_state, material_kinds, axial_diffusivity_by_kind, crosswise_diffusivity_by_kind):
    line_coef = axial_diffusivity_by_kind[material_kinds]
    ydir_coupling_weight = crosswise_diffusivity_by_kind[0][material_kinds]
    zdir_coupling_weight = crosswise_diffusivity_by_kind[1][material_kinds]
    border_extents = ((0, 0), (1, 1), (1, 1))
    bordered_thermal_state = jnp.pad(thermal_state, border_extents)
    bordered_ydir_kinds = jnp.pad(ydir_coupling_weight, border_extents)
    bordered_zdir_kinds = jnp.pad(zdir_coupling_weight, border_extents)
    north_flux_weight = (ydir_coupling_weight + bordered_ydir_kinds[:, 2:, 1:-1]) * 0.5
    south_flux_weight = (ydir_coupling_weight + bordered_ydir_kinds[:, :-2, 1:-1]) * 0.5
    ceiling_flux_weight = (zdir_coupling_weight + bordered_zdir_kinds[:, 1:-1, 2:]) * 0.5
    bottom_flux_weight = (zdir_coupling_weight + bordered_zdir_kinds[:, 1:-1, :-2]) * 0.5
    thermal_forcing_rhs = (thermal_state + north_flux_weight * (bordered_thermal_state[:, 2:, 1:-1] - thermal_state)
              - south_flux_weight * (thermal_state - bordered_thermal_state[:, :-2, 1:-1])
              + ceiling_flux_weight * (bordered_thermal_state[:, 1:-1, 2:] - thermal_state)
              - bottom_flux_weight * (thermal_state - bordered_thermal_state[:, 1:-1, :-2]))
    padded_x = jnp.pad(line_coef, ((1, 1), (0, 0), (0, 0)))
    faces = (padded_x[:-1] + padded_x[1:]) * 0.5
    main_band = 1.0 + faces[:-1] + faces[1:]
    result = solve_lines(-faces[:-1], main_band, -faces[1:], thermal_forcing_rhs[:, None])
    return result[:, 0]
```

```python
import functools

import jax
import jax.numpy as jnp
from jax import lax
from jax.experimental import pallas as pl
from jax.experimental.pallas import tpu as pltpu
from jax.sharding import PartitionSpec as P

F32 = jnp.float32
LANES = 128
GROUP = 8
VMEM_LIMIT = 8 * 1024 * 1024
CHUNKS = 4
BLOCK = 8
SMEM_SPEC = pl.BlockSpec(memory_space=pltpu.SMEM)
VMEM_SPEC = pl.BlockSpec(memory_space=pltpu.VMEM)
ANY_SPEC = pl.BlockSpec(memory_space=pl.ANY)


def iota(shape, axis):
    return lax.broadcasted_iota(jnp.int32, shape, axis)


def half_table(table, row, classes):
    return [(table[c] if row is None else table[row, c]) * 0.5 for c in range(classes)]


def masks(kinds):
    return kinds >= 4, (kinds & 2) != 0, (kinds & 1) != 0


def choose(table, bits):
    level = list(table)
    for bit in bits:
        half = len(level) // 2
        level = [jnp.where(bit, high, low) for low, high in zip(level[:half], level[half:])]
    return level[0]


def pick(table, kinds):
    return choose(table, masks(kinds))


def pick_two(first, second, kinds):
    bits = masks(kinds)
    return choose(first, bits), choose(second, bits)


def reciprocal(x):
    r = pl.reciprocal(x, approx=True)
    return r * (2.0 - x * r)


def faces_kernel(nx, ny, cross, u_hbm, kind_hbm, u_ref, kind_ref, ya_ref, yb_ref, z_ref, k_pack, sems):
    step = nx // CHUNKS
    copies = []
    for c in range(CHUNKS):
        part = pl.ds(c * step, step)
        pair = (
            pltpu.make_async_copy(u_hbm.at[part], u_ref.at[part], sems.at[0, c]),
            pltpu.make_async_copy(kind_hbm.at[part], kind_ref.at[part], sems.at[1, c]),
        )
        for copy in pair:
            copy.start()
        copies.append(pair)
    classes = cross.shape[1]
    ky = half_table(cross, 0, classes)
    kz = half_table(cross, 1, classes)
    even = lax.axis_index("gy") % 2 == 0
    inner = jnp.where(lax.axis_index("gz") == 0, LANES - 1, 0)
    lane = iota((GROUP, LANES), 1)
    for c in range(CHUNKS):
        for copy in copies[c]:
            copy.wait()
        for g in range(ny // GROUP):
            rows = pl.ds(g * GROUP, GROUP)
            u_pack = jnp.zeros((GROUP, LANES), F32) if c == 0 else z_ref[rows]
            kinds = jnp.zeros((GROUP, LANES), jnp.int32) if c == 0 else k_pack[rows]
            for i in range(c * step, (c + 1) * step):
                shift = lax.rem(LANES + i - inner, LANES)
                u_pack = jnp.where(lane == i, pltpu.roll(u_ref[i, rows], shift, 1), u_pack)
                kinds = jnp.where(lane == i, pltpu.roll(kind_ref[i, rows], shift, 1), kinds)
            if c < CHUNKS - 1:
                z_ref[rows], k_pack[rows] = u_pack, kinds
            else:
                hz = pltpu.roll(pick(kz, kinds), nx, 1)
                z_ref[rows] = jnp.where(lane < nx, u_pack, hz)
    u_top, u_bottom = u_ref[:, ny - 1, :], u_ref[:, 0, :]
    k_top, k_bottom = pick(ky, kind_ref[:, ny - 1, :]), pick(ky, kind_ref[:, 0, :])
    ya_ref[0] = jnp.where(even, u_top, u_bottom)
    ya_ref[1] = jnp.where(even, k_top, k_bottom)
    yb_ref[0] = jnp.where(even, u_bottom, u_top)
    yb_ref[1] = jnp.where(even, k_bottom, k_top)


def source_kernel(nx, ny, cross, u_ref, kind_ref, s_ref):
    classes = cross.shape[1]
    ky = half_table(cross, 0, classes)
    kz = half_table(cross, 1, classes)
    core = lax.axis_index("gz")
    lane = iota((GROUP, LANES), 1)
    row = iota((GROUP, LANES), 0)
    last_lane = lane == LANES - 1
    outer = lane == jnp.where(core == 0, 0, LANES - 1)
    groups = ny // GROUP

    for i in range(nx):
        def fetch(g):
            u = u_ref[i, pl.ds(g * GROUP, GROUP)]
            hy, hz = pick_two(ky, kz, kind_ref[i, pl.ds(g * GROUP, GROUP)])
            return u, hz, hy, pltpu.roll(u, GROUP - 1, 0), pltpu.roll(hy, GROUP - 1, 0)

        now = fetch(0)
        below = jnp.zeros((GROUP, LANES), F32)
        for g in range(groups):
            u, hz, hy, u_rolled, hy_rolled = now
            if g < groups - 1:
                now = fetch(g + 1)
                u_up = jnp.where(row == GROUP - 1, now[3], u_rolled)
                hy_up = jnp.where(row == GROUP - 1, now[4], hy_rolled)
                flux = (hy + hy_up) * (u_up - u)
            else:
                flux = jnp.where(row == GROUP - 1, 0.0, (hy + hy_rolled) * (u_rolled - u))
            down = pltpu.roll(flux, 1, 0)
            total = u + flux - jnp.where(row == 0, below, down)
            below = down
            z_flux = (hz + pltpu.roll(hz, LANES - 1, 1)) * (pltpu.roll(u, LANES - 1, 1) - u)
            z_down = (hz + pltpu.roll(hz, 1, 1)) * (u - pltpu.roll(u, 1, 1))
            total = total + (jnp.where(last_lane, 0.0, z_flux) - jnp.where(lane == 0, 0.0, z_down))
            s_ref[i, pl.ds(g * GROUP, GROUP)] = jnp.where(outer, total - hz * u, total)


def sweep_kernel(
    nx, ny, axial, ya, yb, z, ya_in, yb_in, z_in, kind_ref, s_ref, t_ref, e_ref, q_ref, send_ref, top, bottom
):
    at, last = lax.axis_index("gy"), lax.axis_size("gy") - 1
    even = at % 2 == 0
    core = lax.axis_index("gz")

    def edge(own, other, inside):
        keep = jnp.where(inside, 1.0, 0.0)
        return (own[1] + other[1] * keep) * (other[0] * keep - own[0])

    has_up, has_down = at < last, at > 0
    flux_a = edge(ya, ya_in, jnp.where(even, has_up, has_down))
    flux_b = edge(yb, yb_in, jnp.where(even, has_down, has_up))
    top[...] = jnp.where(even, flux_a, flux_b)
    bottom[...] = jnp.where(even, flux_b, flux_a)
    kx = half_table(axial, None, axial.shape[0])
    inner = iota((GROUP, LANES), 1) == jnp.where(core == 0, LANES - 1, 0)
    row = iota((GROUP, LANES), 0)
    block = BLOCK
    blocks = ny // GROUP // block

    @pl.loop(0, blocks)
    def _(b):
        def rows(g):
            return pl.ds(pl.multiple_of((b * block + g) * GROUP, GROUP), GROUP)

        z_flux = []
        for g in range(block):
            own, other = z[rows(g)], z_in[rows(g)]
            z_flux.append(pltpu.roll(own + other, LANES - nx, 1) * (other - own))
        low = jnp.where(b == 0, 1.0, 0.0)
        high = jnp.where(b == blocks - 1, 1.0, 0.0)

        def source(i, g):
            s = s_ref[i, rows(g)]
            s = jnp.where(inner, s + jnp.broadcast_to(z_flux[g][:, i : i + 1], s.shape), s)
            if g == 0:
                s = jnp.where(row == 0, s + low * bottom[i : i + 1, :], s)
            if g == block - 1:
                s = jnp.where(row == GROUP - 1, s + high * top[i : i + 1, :], s)
            return s

        one = jnp.ones((GROUP, LANES), F32)
        state = []
        for g in range(block):
            first, here = pick(kx, kind_ref[0, rows(g)]), pick(kx, kind_ref[1, rows(g)])
            send_ref[b * block + g, 3] = first
            state.append((one, first + here, one, here, source(0, g), source(1, g)))
        for i in range(1, nx - 1):
            for g in range(block):
                first_ground, mutual, ground, here, first_value, value = state[g]
                after = pick(kx, kind_ref[i + 1, rows(g)])
                face = here + after
                r = reciprocal(ground + (mutual + face))
                t = face * r
                e = mutual * r
                t_ref[i, rows(g)] = t
                e_ref[i, rows(g)] = e
                q_ref[i, rows(g)] = value * r
                state[g] = (
                    first_ground + e * ground,
                    mutual * t,
                    1.0 + t * ground,
                    after,
                    first_value + e * value,
                    source(i + 1, g) + t * value,
                )
        for g in range(block):
            first_ground, mutual, ground, here, first_value, value = state[g]
            for n, item in zip((0, 1, 2, 4, 5, 6), (first_ground, mutual, ground, here, first_value, value)):
                send_ref[b * block + g, n] = item


def reduced_kernel(parts, got, out):
    half = parts // 2

    def inward(order, head):
        ends = (0, 2, 3, 4, 5, 6) if head else (2, 0, 4, 3, 6, 5)
        near, far, near_k, far_k, near_y, far_y = ends
        state = None
        steps = []
        for p in order:
            ground, value = got[p, near], got[p, near_y]
            joint = None
            if state is None:
                ground = ground + got[p, near_k]
            else:
                g, y, k = state
                face = k + got[p, near_k]
                r = reciprocal(g + face)
                t = face * r
                joint = (y * r, t)
                ground, value = ground + t * g, value + t * y
            m = got[p, 1]
            r = reciprocal(ground + m)
            t = m * r
            steps.append((p, joint, (value * r, t)))
            state = (got[p, far] + t * ground, got[p, far_y] + t * value, got[p, far_k])
        return state, steps

    left, left_steps = inward(range(half), True)
    right, right_steps = inward(range(parts - 1, half - 1, -1), False)
    face = left[2] + right[2]
    r = reciprocal(left[0] + face)
    t = face * r
    right_end = (right[1] + t * left[1]) * reciprocal(right[0] + t * left[0])
    left_end = left[1] * r + t * right_end

    def outward(steps, value, near, far):
        for p, joint, (base, slope) in reversed(steps):
            out[p, far] = value
            value = base + slope * value
            out[p, near] = value
            if joint is not None:
                value = joint[0] + joint[1] * value

    outward(left_steps, left_end, 0, 1)
    outward(right_steps, right_end, 1, 0)


def back_kernel(nx, ny, ends, q_ref, t_ref, e_ref, out_hbm, out, sems):
    block = 4
    count = ny // GROUP // block
    copies = []
    for b in range(count):

        def rows(g):
            return pl.ds((b * block + g) * GROUP, GROUP)

        head = [ends[b * block + g, 0] for g in range(block)]
        value = [ends[b * block + g, 1] for g in range(block)]
        for g in range(block):
            out[0, rows(g)] = head[g]
            out[nx - 1, rows(g)] = value[g]
        for i in range(nx - 2, 0, -1):
            for g in range(block):
                known = q_ref[i, rows(g)] + e_ref[i, rows(g)] * head[g]
                value[g] = known + t_ref[i, rows(g)] * value[g]
                out[i, rows(g)] = value[g]
        part = pl.ds(b * block * GROUP, block * GROUP)
        copy = pltpu.make_async_copy(out.at[:, part], out_hbm.at[:, part], sems.at[b])
        copy.start()
        copies.append(copy)
    for copy in copies:
        copy.wait()


def near(x):
    return pltpu.with_memory_space_constraint(x, pltpu.VMEM)


def far(x):
    return pltpu.with_memory_space_constraint(x, pltpu.HBM)


def call(kernel, name, outs, in_specs, out_specs, scratch=(), cost=(0, 0)):
    return pl.pallas_call(
        kernel,
        name=name,
        out_shape=outs,
        in_specs=in_specs,
        out_specs=out_specs,
        scratch_shapes=list(scratch),
        compiler_params=pltpu.CompilerParams(vmem_limit_bytes=VMEM_LIMIT),
        cost_estimate=pl.CostEstimate(flops=cost[0], bytes_accessed=cost[1], transcendentals=0),
    )


def per_device(u, kinds, axial, cross):
    nx, ny, nz = u.shape
    parts = lax.axis_size("gx")
    rows_of_y = lax.axis_size("gy")
    groups = ny // GROUP
    cells = nx * ny * nz
    field = pltpu.VMEM((nx, ny, nz), F32)
    y_face = pltpu.VMEM((2, nx, nz), F32)
    z_face = pltpu.VMEM((ny, LANES), F32)
    u_here, kind_here, ya, yb, z = call(
        functools.partial(faces_kernel, nx, ny),
        "faces",
        (field, pltpu.VMEM((nx, ny, nz), jnp.int32), y_face, y_face, z_face),
        [SMEM_SPEC, ANY_SPEC, ANY_SPEC],
        (VMEM_SPEC,) * 5,
        [pltpu.VMEM((ny, LANES), jnp.int32), pltpu.SemaphoreType.DMA((2, CHUNKS))],
        (2 * cells, 8 * cells),
    )(cross, far(u), far(kinds))
    odd_pairs = [(i, i ^ 1) for i in range(rows_of_y)]
    even_pairs = [(i, (i + 1 if i % 2 else i - 1) % rows_of_y) for i in range(rows_of_y)]
    ya_in = lax.ppermute(ya, "gy", odd_pairs)
    yb_in = lax.ppermute(yb, "gy", even_pairs)
    z_in = lax.ppermute(z, "gz", [(0, 1), (1, 0)])
    kind_here = near(kind_here)
    s = call(
        functools.partial(source_kernel, nx, ny),
        "source",
        field,
        [SMEM_SPEC, VMEM_SPEC, VMEM_SPEC],
        VMEM_SPEC,
        cost=(60 * cells, 8 * cells),
    )(cross, near(u_here), kind_here)
    t, e, q, send = call(
        functools.partial(sweep_kernel, nx, ny),
        "sweep",
        (field, field, field, pltpu.VMEM((groups, 7, GROUP, LANES), F32)),
        [SMEM_SPEC] + [VMEM_SPEC] * 8,
        (VMEM_SPEC,) * 4,
        [pltpu.VMEM((nx, nz), F32), pltpu.VMEM((nx, nz), F32)],
        (40 * cells, 8 * cells),
    )(axial, *map(near, (ya, yb, z, ya_in, yb_in, z_in, kind_here, s)))
    got = lax.all_to_all(send, "gx", 0, 0, tiled=True)
    solved = call(
        functools.partial(reduced_kernel, parts),
        "reduced",
        pltpu.VMEM((parts, 2, GROUP, LANES), F32),
        [VMEM_SPEC],
        VMEM_SPEC,
    )(near(got))
    ends = lax.all_to_all(solved, "gx", 0, 0, tiled=True)
    return call(
        functools.partial(back_kernel, nx, ny),
        "back",
        jax.ShapeDtypeStruct((nx, ny, nz), F32),
        [VMEM_SPEC] * 4,
        ANY_SPEC,
        [pltpu.VMEM((nx, ny, nz), F32), pltpu.SemaphoreType.DMA((ny // GROUP // 4,))],
        (4 * cells, 8 * cells),
    )(*map(near, (ends, q, t, e)))


def solution(mesh):
    placed = (P("gx", "gy", "gz"), P("gx", "gy", "gz"), P(), P())
    return jax.shard_map(
        per_device, mesh=mesh, in_specs=placed, out_specs=P("gx", "gy", "gz"), check_vma=False
    )
```

```python
import functools

import jax
import jax.numpy as jnp
from jax import lax
from jax.experimental import pallas as pl
from jax.experimental.pallas import tpu as pltpu
from jax.sharding import PartitionSpec as P

F32 = jnp.float32
LANES = 128
GROUP = 8
VMEM_LIMIT = 12 * 1024 * 1024
CHUNKS = 8
BLOCK = 16
SMEM_SPEC = pl.BlockSpec(memory_space=pltpu.SMEM)
VMEM_SPEC = pl.BlockSpec(memory_space=pltpu.VMEM)
ANY_SPEC = pl.BlockSpec(memory_space=pl.ANY)


def iota(shape, axis):
    return lax.broadcasted_iota(jnp.int32, shape, axis)


def half_table(table, row, classes):
    return [(table[c] if row is None else table[row, c]) * 0.5 for c in range(classes)]


def choose(table, bits):
    level = list(table)
    for bit in bits:
        half = len(level) // 2
        level = [jnp.where(bit, high, low) for low, high in zip(level[:half], level[half:])]
    return level[0]


def pick(tables, kinds):
    bits = kinds >= 4, (kinds & 2) != 0, (kinds & 1) != 0
    return [choose(table, bits) for table in tables]


def reciprocal(x):
    r = pl.reciprocal(x, approx=True)
    return r * (2.0 - x * r)


def local_kernel(
    nx, ny, axial_hbm, cross_hbm, u_hbm, kind_hbm, s_ref, x_ref, ya_ref, yb_ref, z_ref,
    u_ref, kind_ref, axial, cross, sems, table_sems,
):
    table_copies = [
        pltpu.make_async_copy(axial_hbm, axial, table_sems.at[0]),
        pltpu.make_async_copy(cross_hbm, cross, table_sems.at[1]),
    ]
    for copy in table_copies:
        copy.start()
    step = nx // CHUNKS
    copies = []
    for c in range(CHUNKS):
        part = pl.ds(c * step, step)
        pair = (
            pltpu.make_async_copy(kind_hbm.at[part], kind_ref.at[part], sems.at[1, c]),
            pltpu.make_async_copy(u_hbm.at[part], u_ref.at[part], sems.at[0, c]),
        )
        for copy in pair:
            copy.start()
        copies.append(pair)
    for copy in table_copies:
        copy.wait()
    classes = axial.shape[0]
    kx = half_table(axial, None, classes)
    ky = half_table(cross, 0, classes)
    kz = half_table(cross, 1, classes)
    even = lax.axis_index("gy") % 2 == 0
    core = lax.axis_index("gz")
    inner = jnp.where(core == 0, LANES - 1, 0)
    lane = iota((GROUP, LANES), 1)
    row = iota((GROUP, LANES), 0)
    outer = lane == LANES - 1 - inner
    groups = ny // GROUP

    def fetch(i, g):
        rows = pl.ds(g * GROUP, GROUP)
        u = u_ref[i, rows]
        hx, hy, hz = pick((kx, ky, kz), kind_ref[i, rows])
        x_ref[i, rows] = hx
        return u, hz, hy, pltpu.roll(u, GROUP - 1, 0), pltpu.roll(hy, GROUP - 1, 0)

    for i in range(nx):
        if i % step == 0:
            for copy in copies[i // step]:
                copy.wait()
        shift = lax.rem(LANES + i - inner, LANES)
        shift_k = lax.rem(LANES + nx + i - inner, LANES)
        now = fetch(i, 0)
        below = jnp.zeros((GROUP, LANES), F32)
        for g in range(groups):
            u, hz, hy, u_rolled, hy_rolled = now
            if g < groups - 1:
                now = fetch(i, g + 1)
                u_up = jnp.where(row == GROUP - 1, now[3], u_rolled)
                hy_up = jnp.where(row == GROUP - 1, now[4], hy_rolled)
                flux = (hy + hy_up) * (u_up - u)
            else:
                flux = jnp.where(row == GROUP - 1, 0.0, (hy + hy_rolled) * (u_rolled - u))
            down = pltpu.roll(flux, 1, 0)
            total = u + flux - jnp.where(row == 0, below, down)
            below = down
            z_up = (hz + pltpu.roll(hz, LANES - 1, 1)) * (pltpu.roll(u, LANES - 1, 1) - u)
            z_down = (hz + pltpu.roll(hz, 1, 1)) * (u - pltpu.roll(u, 1, 1))
            total = total + (jnp.where(lane == LANES - 1, 0.0, z_up) - jnp.where(lane == 0, 0.0, z_down))
            rows = pl.ds(g * GROUP, GROUP)
            s_ref[i, rows] = jnp.where(outer, total - hz * u, total)
            packed = z_ref[rows] if i else jnp.zeros((GROUP, LANES), F32)
            packed = jnp.where(lane == i, pltpu.roll(u, shift, 1), packed)
            z_ref[rows] = jnp.where(lane == nx + i, pltpu.roll(hz, shift_k, 1), packed)
    u_top, u_bottom = u_ref[:, ny - 1, :], u_ref[:, 0, :]
    k_top, k_bottom = pick((ky,), kind_ref[:, ny - 1, :])[0], pick((ky,), kind_ref[:, 0, :])[0]
    ya_ref[0] = jnp.where(even, u_top, u_bottom)
    ya_ref[1] = jnp.where(even, k_top, k_bottom)
    yb_ref[0] = jnp.where(even, u_bottom, u_top)
    yb_ref[1] = jnp.where(even, k_bottom, k_top)


def coefficients_kernel(nx, ny, x_ref, t_ref, e_ref, r_ref, net_ref):
    for b in range(ny // GROUP // BLOCK):

        def rows(g):
            return pl.ds((b * BLOCK + g) * GROUP, GROUP)

        one = jnp.ones((GROUP, LANES), F32)
        state = []
        for g in range(BLOCK):
            first, here = x_ref[0, rows(g)], x_ref[1, rows(g)]
            net_ref[b * BLOCK + g, 3] = first
            state.append((one, first + here, one, here))
        for i in range(1, nx - 1):
            for g in range(BLOCK):
                first_ground, mutual, ground, here = state[g]
                after = x_ref[i + 1, rows(g)]
                face = here + after
                r = reciprocal(ground + (mutual + face))
                t = face * r
                e = mutual * r
                t_ref[i, rows(g)] = t
                e_ref[i, rows(g)] = e
                r_ref[i, rows(g)] = r
                state[g] = (first_ground + e * ground, mutual * t, 1.0 + t * ground, after)
        for g in range(BLOCK):
            for n, item in zip((0, 1, 2, 4), state[g]):
                net_ref[b * BLOCK + g, n] = item


def forward_kernel(
    nx, ny, ya, yb, z, ya_in, yb_in, z_in, s_ref, t_ref, e_ref, r_ref, net_ref, q_ref, send_ref, top, bottom
):
    at, last = lax.axis_index("gy"), lax.axis_size("gy") - 1
    even = at % 2 == 0
    core = lax.axis_index("gz")

    def edge(own, other, inside):
        keep = jnp.where(inside, 1.0, 0.0)
        return (own[1] + other[1] * keep) * (other[0] * keep - own[0])

    has_up, has_down = at < last, at > 0
    flux_a = edge(ya, ya_in, jnp.where(even, has_up, has_down))
    flux_b = edge(yb, yb_in, jnp.where(even, has_down, has_up))
    top[...] = jnp.where(even, flux_a, flux_b)
    bottom[...] = jnp.where(even, flux_b, flux_a)
    inner = iota((GROUP, LANES), 1) == jnp.where(core == 0, LANES - 1, 0)
    row = iota((GROUP, LANES), 0)
    blocks = ny // GROUP // BLOCK
    for b in range(blocks):

        def rows(g):
            return pl.ds((b * BLOCK + g) * GROUP, GROUP)

        z_flux = []
        for g in range(BLOCK):
            own, other = z[rows(g)], z_in[rows(g)]
            z_flux.append(pltpu.roll(own + other, LANES - nx, 1) * (other - own))

        def source(i, g):
            s = s_ref[i, rows(g)]
            s = jnp.where(inner, s + jnp.broadcast_to(z_flux[g][:, i : i + 1], s.shape), s)
            if b == 0 and g == 0:
                s = jnp.where(row == 0, s + bottom[i : i + 1, :], s)
            if b == blocks - 1 and g == BLOCK - 1:
                s = jnp.where(row == GROUP - 1, s + top[i : i + 1, :], s)
            return s

        first = [source(0, g) for g in range(BLOCK)]
        value = [source(1, g) for g in range(BLOCK)]
        for i in range(1, nx - 1):
            for g in range(BLOCK):
                q_ref[i, rows(g)] = r_ref[i, rows(g)] * value[g]
                first[g] = first[g] + e_ref[i, rows(g)] * value[g]
                value[g] = source(i + 1, g) + t_ref[i, rows(g)] * value[g]
        for g in range(BLOCK):
            for n in range(5):
                send_ref[b * BLOCK + g, n] = net_ref[b * BLOCK + g, n]
            send_ref[b * BLOCK + g, 5] = first[g]
            send_ref[b * BLOCK + g, 6] = value[g]


def reduced_kernel(parts, got, out):
    half = parts // 2

    def inward(order, head):
        ends = (0, 2, 3, 4, 5, 6) if head else (2, 0, 4, 3, 6, 5)
        near, far, near_k, far_k, near_y, far_y = ends
        state = None
        steps = []
        for p in order:
            ground, value = got[p, near], got[p, near_y]
            joint = None
            if state is None:
                ground = ground + got[p, near_k]
            else:
                g, y, k = state
                face = k + got[p, near_k]
                r = reciprocal(g + face)
                t = face * r
                joint = (y * r, t)
                ground, value = ground + t * g, value + t * y
            m = got[p, 1]
            r = reciprocal(ground + m)
            t = m * r
            steps.append((p, joint, (value * r, t)))
            state = (got[p, far] + t * ground, got[p, far_y] + t * value, got[p, far_k])
        return state, steps

    left, left_steps = inward(range(half), True)
    right, right_steps = inward(range(parts - 1, half - 1, -1), False)
    face = left[2] + right[2]
    r = reciprocal(left[0] + face)
    t = face * r
    right_end = (right[1] + t * left[1]) * reciprocal(right[0] + t * left[0])
    left_end = left[1] * r + t * right_end

    def outward(steps, value, near, far):
        for p, joint, (base, slope) in reversed(steps):
            out[p, far] = value
            value = base + slope * value
            out[p, near] = value
            if joint is not None:
                value = joint[0] + joint[1] * value

    outward(left_steps, left_end, 0, 1)
    outward(right_steps, right_end, 1, 0)


def back_kernel(nx, ny, ends, q_ref, t_ref, e_ref, out_hbm, out, sems):
    block = 4
    count = ny // GROUP // block
    copies = []
    for b in range(count):

        def rows(g):
            return pl.ds((b * block + g) * GROUP, GROUP)

        head = [ends[b * block + g, 0] for g in range(block)]
        value = [ends[b * block + g, 1] for g in range(block)]
        for g in range(block):
            out[0, rows(g)] = head[g]
            out[nx - 1, rows(g)] = value[g]
        for i in range(nx - 2, 0, -1):
            for g in range(block):
                known = q_ref[i, rows(g)] + e_ref[i, rows(g)] * head[g]
                value[g] = known + t_ref[i, rows(g)] * value[g]
                out[i, rows(g)] = value[g]
        part = pl.ds(b * block * GROUP, block * GROUP)
        copy = pltpu.make_async_copy(out.at[:, part], out_hbm.at[:, part], sems.at[b])
        copy.start()
        copies.append(copy)
    for copy in copies:
        copy.wait()


def near(x):
    return pltpu.with_memory_space_constraint(x, pltpu.VMEM)


def far(x):
    return pltpu.with_memory_space_constraint(x, pltpu.HBM)


def call(kernel, name, outs, in_specs, out_specs, scratch=(), cost=(0, 0)):
    return pl.pallas_call(
        kernel,
        name=name,
        out_shape=outs,
        in_specs=in_specs,
        out_specs=out_specs,
        scratch_shapes=list(scratch),
        compiler_params=pltpu.CompilerParams(vmem_limit_bytes=VMEM_LIMIT),
        cost_estimate=pl.CostEstimate(flops=cost[0], bytes_accessed=cost[1], transcendentals=0),
    )


def per_device(u, kinds, axial, cross):
    nx, ny, nz = u.shape
    parts = lax.axis_size("gx")
    rows_of_y = lax.axis_size("gy")
    groups = ny // GROUP
    cells = nx * ny * nz
    field = pltpu.VMEM((nx, ny, nz), F32)
    y_face = pltpu.VMEM((2, nx, nz), F32)
    z_face = pltpu.VMEM((ny, LANES), F32)
    s, x, ya, yb, z = call(
        functools.partial(local_kernel, nx, ny),
        "local",
        (field, field, y_face, y_face, z_face),
        [ANY_SPEC] * 4,
        (VMEM_SPEC,) * 5,
        [
            pltpu.VMEM((nx, ny, nz), F32),
            pltpu.VMEM((nx, ny, nz), jnp.int32),
            pltpu.SMEM(axial.shape, F32),
            pltpu.SMEM(cross.shape, F32),
            pltpu.SemaphoreType.DMA((2, CHUNKS)),
            pltpu.SemaphoreType.DMA((2,)),
        ],
        (60 * cells, 8 * cells),
    )(*map(far, (axial, cross, u, kinds)))
    odd_pairs = [(i, i ^ 1) for i in range(rows_of_y)]
    even_pairs = [(i, (i + 1 if i % 2 else i - 1) % rows_of_y) for i in range(rows_of_y)]
    ya_in = lax.ppermute(ya, "gy", odd_pairs)
    yb_in = lax.ppermute(yb, "gy", even_pairs)
    z_in = lax.ppermute(z, "gz", [(0, 1), (1, 0)])
    t, e, r, net = call(
        functools.partial(coefficients_kernel, nx, ny),
        "coefficients",
        (field, field, field, pltpu.VMEM((groups, 5, GROUP, LANES), F32)),
        [VMEM_SPEC],
        (VMEM_SPEC,) * 4,
        cost=(80 * cells, 8 * cells),
    )(near(x))
    q, send = call(
        functools.partial(forward_kernel, nx, ny),
        "forward",
        (field, pltpu.VMEM((groups, 7, GROUP, LANES), F32)),
        [VMEM_SPEC] * 11,
        (VMEM_SPEC,) * 2,
        [pltpu.VMEM((nx, nz), F32), pltpu.VMEM((nx, nz), F32)],
        (10 * cells, 8 * cells),
    )(*map(near, (ya, yb, z, ya_in, yb_in, z_in, s, t, e, r, net)))
    got = lax.all_to_all(send, "gx", 0, 0, tiled=True)
    solved = call(
        functools.partial(reduced_kernel, parts),
        "reduced",
        pltpu.VMEM((parts, 2, GROUP, LANES), F32),
        [VMEM_SPEC],
        VMEM_SPEC,
    )(near(got))
    ends = lax.all_to_all(solved, "gx", 0, 0, tiled=True)
    return call(
        functools.partial(back_kernel, nx, ny),
        "back",
        jax.ShapeDtypeStruct((nx, ny, nz), F32),
        [VMEM_SPEC] * 4,
        ANY_SPEC,
        [pltpu.VMEM((nx, ny, nz), F32), pltpu.SemaphoreType.DMA((ny // GROUP // 4,))],
        (4 * cells, 8 * cells),
    )(*map(near, (ends, q, t, e)))


def solution(mesh):
    placed = (P("gx", "gy", "gz"), P("gx", "gy", "gz"), P(), P())
    return jax.shard_map(
        per_device, mesh=mesh, in_specs=placed, out_specs=P("gx", "gy", "gz"), check_vma=False
    )
```

```python
import functools

import jax
import jax.numpy as jnp
from jax import lax
from jax.experimental import pallas as pl
from jax.experimental.pallas import tpu as pltpu
from jax.sharding import PartitionSpec as P

F32 = jnp.float32
LANES = 128
GROUP = 8
VMEM_LIMIT = 12 * 1024 * 1024
CHUNKS = 8
BLOCK = 16
SMEM_SPEC = pl.BlockSpec(memory_space=pltpu.SMEM)
VMEM_SPEC = pl.BlockSpec(memory_space=pltpu.VMEM)
ANY_SPEC = pl.BlockSpec(memory_space=pl.ANY)


def iota(shape, axis):
    return lax.broadcasted_iota(jnp.int32, shape, axis)


def half_table(table, row, classes):
    return [(table[c] if row is None else table[row, c]) * 0.5 for c in range(classes)]


def choose(table, bits):
    level = list(table)
    for bit in bits:
        half = len(level) // 2
        level = [jnp.where(bit, high, low) for low, high in zip(level[:half], level[half:])]
    return level[0]


def pick(tables, kinds):
    bits = kinds >= 4, (kinds & 2) != 0, (kinds & 1) != 0
    return [choose(table, bits) for table in tables]


def reciprocal(x):
    r = pl.reciprocal(x, approx=True)
    return r * (2.0 - x * r)


def local_kernel(
    nx, ny, axial_hbm, cross_hbm, u_hbm, kind_hbm,
    u_ref, hy_ref, hz_ref, t_ref, e_ref, r_ref, net_ref, ya_ref, yb_ref, z_ref,
    kind_ref, axial, cross, sems, table_sems,
):
    table_copies = [
        pltpu.make_async_copy(axial_hbm, axial, table_sems.at[0]),
        pltpu.make_async_copy(cross_hbm, cross, table_sems.at[1]),
    ]
    for copy in table_copies:
        copy.start()
    step = nx // CHUNKS
    copies = []
    for c in range(CHUNKS):
        part = pl.ds(c * step, step)
        pair = (
            pltpu.make_async_copy(kind_hbm.at[part], kind_ref.at[part], sems.at[1, c]),
            pltpu.make_async_copy(u_hbm.at[part], u_ref.at[part], sems.at[0, c]),
        )
        for copy in pair:
            copy.start()
        copies.append(pair)
    for copy in table_copies:
        copy.wait()
    classes = axial.shape[0]
    kx = half_table(axial, None, classes)
    ky = half_table(cross, 0, classes)
    kz = half_table(cross, 1, classes)
    even = lax.axis_index("gy") % 2 == 0
    inner = jnp.where(lax.axis_index("gz") == 0, LANES - 1, 0)
    lane = iota((GROUP, LANES), 1)
    groups = ny // GROUP
    one = jnp.ones((GROUP, LANES), F32)
    state = [None] * groups
    for i in range(nx):
        if i % step == 0:
            for copy in copies[i // step]:
                copy.wait()
        shift = lax.rem(LANES + i - inner, LANES)
        shift_k = lax.rem(LANES + nx + i - inner, LANES)
        for g in range(groups):
            rows = pl.ds(g * GROUP, GROUP)
            after, hy, hz = pick((kx, ky, kz), kind_ref[i, rows])
            hy_ref[i, rows] = hy
            hz_ref[i, rows] = hz
            packed = z_ref[rows] if i else jnp.zeros((GROUP, LANES), F32)
            packed = jnp.where(lane == i, pltpu.roll(u_ref[i, rows], shift, 1), packed)
            z_ref[rows] = jnp.where(lane == nx + i, pltpu.roll(hz, shift_k, 1), packed)
            if i == 0:
                net_ref[g, 3] = after
                state[g] = after
            elif i == 1:
                state[g] = (one, state[g] + after, one, after)
            else:
                first_ground, mutual, ground, here = state[g]
                face = here + after
                r = reciprocal(ground + (mutual + face))
                t = face * r
                e = mutual * r
                t_ref[i - 1, rows] = t
                e_ref[i - 1, rows] = e
                r_ref[i - 1, rows] = r
                state[g] = (first_ground + e * ground, mutual * t, 1.0 + t * ground, after)
    for g in range(groups):
        for n, item in zip((0, 1, 2, 4), state[g]):
            net_ref[g, n] = item
    ya_ref[0] = jnp.where(even, u_ref[:, ny - 1, :], u_ref[:, 0, :])
    ya_ref[1] = jnp.where(even, hy_ref[:, ny - 1, :], hy_ref[:, 0, :])
    yb_ref[0] = jnp.where(even, u_ref[:, 0, :], u_ref[:, ny - 1, :])
    yb_ref[1] = jnp.where(even, hy_ref[:, 0, :], hy_ref[:, ny - 1, :])


def source_kernel(nx, ny, u_ref, hy_ref, hz_ref, s_ref):
    lane = iota((GROUP, LANES), 1)
    row = iota((GROUP, LANES), 0)
    outer = lane == jnp.where(lax.axis_index("gz") == 0, 0, LANES - 1)
    groups = ny // GROUP

    def fetch(i, g):
        rows = pl.ds(g * GROUP, GROUP)
        u, hy = u_ref[i, rows], hy_ref[i, rows]
        return u, hy, pltpu.roll(u, GROUP - 1, 0), pltpu.roll(hy, GROUP - 1, 0)

    for i in range(nx):
        now = fetch(i, 0)
        below = jnp.zeros((GROUP, LANES), F32)
        for g in range(groups):
            rows = pl.ds(g * GROUP, GROUP)
            u, hy, u_rolled, hy_rolled = now
            hz = hz_ref[i, rows]
            if g < groups - 1:
                now = fetch(i, g + 1)
                u_up = jnp.where(row == GROUP - 1, now[2], u_rolled)
                hy_up = jnp.where(row == GROUP - 1, now[3], hy_rolled)
                flux = (hy + hy_up) * (u_up - u)
            else:
                flux = jnp.where(row == GROUP - 1, 0.0, (hy + hy_rolled) * (u_rolled - u))
            down = pltpu.roll(flux, 1, 0)
            total = u + flux - jnp.where(row == 0, below, down)
            below = down
            z_up = (hz + pltpu.roll(hz, LANES - 1, 1)) * (pltpu.roll(u, LANES - 1, 1) - u)
            z_down = (hz + pltpu.roll(hz, 1, 1)) * (u - pltpu.roll(u, 1, 1))
            total = total + (jnp.where(lane == LANES - 1, 0.0, z_up) - jnp.where(lane == 0, 0.0, z_down))
            s_ref[i, rows] = jnp.where(outer, total - hz * u, total)


def forward_kernel(
    nx, ny, ya, yb, z, ya_in, yb_in, z_in, s_ref, t_ref, e_ref, r_ref, net_ref, q_ref, send_ref, top, bottom
):
    at, last = lax.axis_index("gy"), lax.axis_size("gy") - 1
    even = at % 2 == 0
    core = lax.axis_index("gz")

    def edge(own, other, inside):
        keep = jnp.where(inside, 1.0, 0.0)
        return (own[1] + other[1] * keep) * (other[0] * keep - own[0])

    has_up, has_down = at < last, at > 0
    flux_a = edge(ya, ya_in, jnp.where(even, has_up, has_down))
    flux_b = edge(yb, yb_in, jnp.where(even, has_down, has_up))
    top[...] = jnp.where(even, flux_a, flux_b)
    bottom[...] = jnp.where(even, flux_b, flux_a)
    inner = iota((GROUP, LANES), 1) == jnp.where(core == 0, LANES - 1, 0)
    row = iota((GROUP, LANES), 0)
    blocks = ny // GROUP // BLOCK
    for b in range(blocks):

        def rows(g):
            return pl.ds((b * BLOCK + g) * GROUP, GROUP)

        z_flux = []
        for g in range(BLOCK):
            own, other = z[rows(g)], z_in[rows(g)]
            z_flux.append(pltpu.roll(own + other, LANES - nx, 1) * (other - own))

        def source(i, g):
            s = s_ref[i, rows(g)]
            s = jnp.where(inner, s + jnp.broadcast_to(z_flux[g][:, i : i + 1], s.shape), s)
            if b == 0 and g == 0:
                s = jnp.where(row == 0, s + bottom[i : i + 1, :], s)
            if b == blocks - 1 and g == BLOCK - 1:
                s = jnp.where(row == GROUP - 1, s + top[i : i + 1, :], s)
            return s

        first = [source(0, g) for g in range(BLOCK)]
        value = [source(1, g) for g in range(BLOCK)]
        for i in range(1, nx - 1):
            for g in range(BLOCK):
                q_ref[i, rows(g)] = r_ref[i, rows(g)] * value[g]
                first[g] = first[g] + e_ref[i, rows(g)] * value[g]
                value[g] = source(i + 1, g) + t_ref[i, rows(g)] * value[g]
        for g in range(BLOCK):
            for n in range(5):
                send_ref[b * BLOCK + g, n] = net_ref[b * BLOCK + g, n]
            send_ref[b * BLOCK + g, 5] = first[g]
            send_ref[b * BLOCK + g, 6] = value[g]


def reduced_kernel(parts, got, out):
    half = parts // 2

    def inward(order, head):
        ends = (0, 2, 3, 4, 5, 6) if head else (2, 0, 4, 3, 6, 5)
        near, far, near_k, far_k, near_y, far_y = ends
        state = None
        steps = []
        for p in order:
            ground, value = got[p, near], got[p, near_y]
            joint = None
            if state is None:
                ground = ground + got[p, near_k]
            else:
                g, y, k = state
                face = k + got[p, near_k]
                r = reciprocal(g + face)
                t = face * r
                joint = (y * r, t)
                ground, value = ground + t * g, value + t * y
            m = got[p, 1]
            r = reciprocal(ground + m)
            t = m * r
            steps.append((p, joint, (value * r, t)))
            state = (got[p, far] + t * ground, got[p, far_y] + t * value, got[p, far_k])
        return state, steps

    left, left_steps = inward(range(half), True)
    right, right_steps = inward(range(parts - 1, half - 1, -1), False)
    face = left[2] + right[2]
    r = reciprocal(left[0] + face)
    t = face * r
    right_end = (right[1] + t * left[1]) * reciprocal(right[0] + t * left[0])
    left_end = left[1] * r + t * right_end

    def outward(steps, value, near, far):
        for p, joint, (base, slope) in reversed(steps):
            out[p, far] = value
            value = base + slope * value
            out[p, near] = value
            if joint is not None:
                value = joint[0] + joint[1] * value

    outward(left_steps, left_end, 0, 1)
    outward(right_steps, right_end, 1, 0)


def back_kernel(nx, ny, ends, q_ref, t_ref, e_ref, out_hbm, out, sems):
    block = 4
    count = ny // GROUP // block
    copies = []
    for b in range(count):

        def rows(g):
            return pl.ds((b * block + g) * GROUP, GROUP)

        head = [ends[b * block + g, 0] for g in range(block)]
        value = [ends[b * block + g, 1] for g in range(block)]
        for g in range(block):
            out[0, rows(g)] = head[g]
            out[nx - 1, rows(g)] = value[g]
        for i in range(nx - 2, 0, -1):
            for g in range(block):
                known = q_ref[i, rows(g)] + e_ref[i, rows(g)] * head[g]
                value[g] = known + t_ref[i, rows(g)] * value[g]
                out[i, rows(g)] = value[g]
        part = pl.ds(b * block * GROUP, block * GROUP)
        copy = pltpu.make_async_copy(out.at[:, part], out_hbm.at[:, part], sems.at[b])
        copy.start()
        copies.append(copy)
    for copy in copies:
        copy.wait()


def near(x):
    return pltpu.with_memory_space_constraint(x, pltpu.VMEM)


def far(x):
    return pltpu.with_memory_space_constraint(x, pltpu.HBM)


def call(kernel, name, outs, in_specs, out_specs, scratch=(), cost=(0, 0)):
    return pl.pallas_call(
        kernel,
        name=name,
        out_shape=outs,
        in_specs=in_specs,
        out_specs=out_specs,
        scratch_shapes=list(scratch),
        compiler_params=pltpu.CompilerParams(vmem_limit_bytes=VMEM_LIMIT),
        cost_estimate=pl.CostEstimate(flops=cost[0], bytes_accessed=cost[1], transcendentals=0),
    )


def per_device(u, kinds, axial, cross):
    nx, ny, nz = u.shape
    parts = lax.axis_size("gx")
    rows_of_y = lax.axis_size("gy")
    groups = ny // GROUP
    cells = nx * ny * nz
    field = pltpu.VMEM((nx, ny, nz), F32)
    y_face = pltpu.VMEM((2, nx, nz), F32)
    z_face = pltpu.VMEM((ny, LANES), F32)
    u_here, hy, hz, t, e, r, net, ya, yb, z = call(
        functools.partial(local_kernel, nx, ny),
        "local",
        (field,) * 6 + (pltpu.VMEM((groups, 5, GROUP, LANES), F32), y_face, y_face, z_face),
        [ANY_SPEC] * 4,
        (VMEM_SPEC,) * 10,
        [
            pltpu.VMEM((nx, ny, nz), jnp.int32),
            pltpu.SMEM(axial.shape, F32),
            pltpu.SMEM(cross.shape, F32),
            pltpu.SemaphoreType.DMA((2, CHUNKS)),
            pltpu.SemaphoreType.DMA((2,)),
        ],
        (60 * cells, 8 * cells),
    )(*map(far, (axial, cross, u, kinds)))
    odd_pairs = [(i, i ^ 1) for i in range(rows_of_y)]
    even_pairs = [
        (2 * i + c, 2 * j + c if 0 <= j < rows_of_y else 2 * i + 1 - c)
        for i in range(rows_of_y)
        for j in (i + 1 if i % 2 else i - 1,)
        for c in range(2)
    ]
    ya_in = lax.ppermute(ya, "gy", odd_pairs)
    yb_in = lax.ppermute(yb, ("gy", "gz"), even_pairs)
    z_in = lax.ppermute(z, "gz", [(0, 1), (1, 0)])
    s = call(
        functools.partial(source_kernel, nx, ny),
        "source",
        field,
        [VMEM_SPEC] * 3,
        VMEM_SPEC,
        cost=(80 * cells, 8 * cells),
    )(*map(near, (u_here, hy, hz)))
    q, send = call(
        functools.partial(forward_kernel, nx, ny),
        "forward",
        (field, pltpu.VMEM((groups, 7, GROUP, LANES), F32)),
        [VMEM_SPEC] * 11,
        (VMEM_SPEC,) * 2,
        [pltpu.VMEM((nx, nz), F32), pltpu.VMEM((nx, nz), F32)],
        (10 * cells, 8 * cells),
    )(*map(near, (ya, yb, z, ya_in, yb_in, z_in, s, t, e, r, net)))
    got = lax.all_to_all(send, "gx", 0, 0, tiled=True)
    solved = call(
        functools.partial(reduced_kernel, parts),
        "reduced",
        pltpu.VMEM((parts, 2, GROUP, LANES), F32),
        [VMEM_SPEC],
        VMEM_SPEC,
    )(near(got))
    ends = lax.all_to_all(solved, "gx", 0, 0, tiled=True)
    return call(
        functools.partial(back_kernel, nx, ny),
        "back",
        jax.ShapeDtypeStruct((nx, ny, nz), F32),
        [VMEM_SPEC] * 4,
        ANY_SPEC,
        [pltpu.VMEM((nx, ny, nz), F32), pltpu.SemaphoreType.DMA((ny // GROUP // 4,))],
        (4 * cells, 8 * cells),
    )(*map(near, (ends, q, t, e)))


def solution(mesh):
    placed = (P("gx", "gy", "gz"), P("gx", "gy", "gz"), P(), P())
    return jax.shard_map(
        per_device, mesh=mesh, in_specs=placed, out_specs=P("gx", "gy", "gz"), check_vma=False
    )
```

```python
import functools

import jax
import jax.numpy as jnp
from jax import lax
from jax.experimental import pallas as pl
from jax.experimental.pallas import tpu as pltpu
from jax.sharding import PartitionSpec as P

F32 = jnp.float32
LANES = 128
GROUP = 8
VMEM_LIMIT = 12 * 1024 * 1024
CHUNKS = 4
BLOCK = 16
SMEM_SPEC = pl.BlockSpec(memory_space=pltpu.SMEM)
VMEM_SPEC = pl.BlockSpec(memory_space=pltpu.VMEM)
ANY_SPEC = pl.BlockSpec(memory_space=pl.ANY)


def iota(shape, axis):
    return lax.broadcasted_iota(jnp.int32, shape, axis)


def half_table(table, row, classes):
    return [(table[c] if row is None else table[row, c]) * 0.5 for c in range(classes)]


def choose(table, bits):
    level = list(table)
    for bit in bits:
        half = len(level) // 2
        level = [jnp.where(bit, high, low) for low, high in zip(level[:half], level[half:])]
    return level[0]


def pick(tables, kinds):
    bits = kinds >= 4, (kinds & 2) != 0, (kinds & 1) != 0
    return [choose(table, bits) for table in tables]


def reciprocal(x):
    r = pl.reciprocal(x, approx=True)
    return r * (2.0 - x * r)


def local_kernel(
    nx, ny, axial_hbm, cross_hbm, u_hbm, kind_hbm,
    u_ref, x_ref, hy_ref, hz_ref, last_ref, ya_ref, yb_ref, z_ref,
    kind_ref, axial, cross, sems, table_sems,
):
    table_copies = [
        pltpu.make_async_copy(axial_hbm, axial, table_sems.at[0]),
        pltpu.make_async_copy(cross_hbm, cross, table_sems.at[1]),
    ]
    for copy in table_copies:
        copy.start()
    step = nx // CHUNKS
    copies = []
    for c in range(CHUNKS):
        part = pl.ds(c * step, step)
        pair = (
            pltpu.make_async_copy(kind_hbm.at[part], kind_ref.at[part], sems.at[1, c]),
            pltpu.make_async_copy(u_hbm.at[part], u_ref.at[part], sems.at[0, c]),
        )
        for copy in pair:
            copy.start()
        copies.append(pair)
    for copy in table_copies:
        copy.wait()
    classes = axial.shape[0]
    kx = half_table(axial, None, classes)
    ky = half_table(cross, 0, classes)
    kz = half_table(cross, 1, classes)
    even = lax.axis_index("gy") % 2 == 0
    inner = jnp.where(lax.axis_index("gz") == 0, LANES - 1, 0)
    lane = iota((GROUP, LANES), 1)
    groups = ny // GROUP
    for i in range(nx):
        if i % step == 0:
            for copy in copies[i // step]:
                copy.wait()
        shift = lax.rem(LANES + i - inner, LANES)
        shift_k = lax.rem(LANES + nx + i - inner, LANES)
        for g in range(groups):
            rows = pl.ds(g * GROUP, GROUP)
            hx, hy, hz = pick((kx, ky, kz), kind_ref[i, rows])
            x_ref[i, rows] = hx
            if i == nx - 1:
                last_ref[rows] = hx
            hy_ref[i, rows] = hy
            hz_ref[i, rows] = hz
            packed = z_ref[rows] if i else jnp.zeros((GROUP, LANES), F32)
            packed = jnp.where(lane == i, pltpu.roll(u_ref[i, rows], shift, 1), packed)
            z_ref[rows] = jnp.where(lane == nx + i, pltpu.roll(hz, shift_k, 1), packed)
    ya_ref[0] = jnp.where(even, u_ref[:, ny - 1, :], u_ref[:, 0, :])
    ya_ref[1] = jnp.where(even, hy_ref[:, ny - 1, :], hy_ref[:, 0, :])
    yb_ref[0] = jnp.where(even, u_ref[:, 0, :], u_ref[:, ny - 1, :])
    yb_ref[1] = jnp.where(even, hy_ref[:, 0, :], hy_ref[:, ny - 1, :])


def source_kernel(nx, ny, u_ref, x_ref, hy_ref, hz_ref, s_ref, t_ref, e_ref, r_ref, net_ref):
    one = jnp.ones((GROUP, LANES), F32)
    state = [None] * (ny // GROUP)
    lane = iota((GROUP, LANES), 1)
    row = iota((GROUP, LANES), 0)
    outer = lane == jnp.where(lax.axis_index("gz") == 0, 0, LANES - 1)
    groups = ny // GROUP

    def fetch(i, g):
        rows = pl.ds(g * GROUP, GROUP)
        u, hy = u_ref[i, rows], hy_ref[i, rows]
        return u, hy, pltpu.roll(u, GROUP - 1, 0), pltpu.roll(hy, GROUP - 1, 0)

    for i in range(nx):
        now = fetch(i, 0)
        below = jnp.zeros((GROUP, LANES), F32)
        for g in range(groups):
            rows = pl.ds(g * GROUP, GROUP)
            u, hy, u_rolled, hy_rolled = now
            hz = hz_ref[i, rows]
            if g < groups - 1:
                now = fetch(i, g + 1)
                u_up = jnp.where(row == GROUP - 1, now[2], u_rolled)
                hy_up = jnp.where(row == GROUP - 1, now[3], hy_rolled)
                flux = (hy + hy_up) * (u_up - u)
            else:
                flux = jnp.where(row == GROUP - 1, 0.0, (hy + hy_rolled) * (u_rolled - u))
            down = pltpu.roll(flux, 1, 0)
            total = u + flux - jnp.where(row == 0, below, down)
            below = down
            z_up = (hz + pltpu.roll(hz, LANES - 1, 1)) * (pltpu.roll(u, LANES - 1, 1) - u)
            z_down = (hz + pltpu.roll(hz, 1, 1)) * (u - pltpu.roll(u, 1, 1))
            total = total + (jnp.where(lane == LANES - 1, 0.0, z_up) - jnp.where(lane == 0, 0.0, z_down))
            s_ref[i, rows] = jnp.where(outer, total - hz * u, total)
            after = x_ref[i, rows]
            if i == 0:
                net_ref[g, 3] = after
                state[g] = after
            elif i == 1:
                state[g] = (one, state[g] + after, one, after)
            else:
                first_ground, mutual, ground, here = state[g]
                face = here + after
                r = reciprocal(ground + (mutual + face))
                t = face * r
                e = mutual * r
                t_ref[i - 1, rows] = t
                e_ref[i - 1, rows] = e
                r_ref[i - 1, rows] = r
                state[g] = (first_ground + e * ground, mutual * t, 1.0 + t * ground, after)
    for g in range(groups):
        for n, item in zip((0, 1, 2, 4), state[g]):
            net_ref[g, n] = item


def forward_kernel(
    nx, ny, left, ya, yb, z, ya_in, yb_in, z_in, s_ref, t_ref, e_ref, r_ref, net_ref,
    q_ref, first_ref, send_ref, top, bottom,
):
    at, last = lax.axis_index("gy"), lax.axis_size("gy") - 1
    even = at % 2 == 0
    core = lax.axis_index("gz")

    def edge(own, other, inside):
        keep = jnp.where(inside, 1.0, 0.0)
        return (own[1] + other[1] * keep) * (other[0] * keep - own[0])

    has_up, has_down = at < last, at > 0
    flux_a = edge(ya, ya_in, jnp.where(even, has_up, has_down))
    flux_b = edge(yb, yb_in, jnp.where(even, has_down, has_up))
    top[...] = jnp.where(even, flux_a, flux_b)
    bottom[...] = jnp.where(even, flux_b, flux_a)
    part, parts = lax.axis_index("gx"), lax.axis_size("gx")
    starts, ends = part == 0, part == parts - 1
    inner = iota((GROUP, LANES), 1) == jnp.where(core == 0, LANES - 1, 0)
    row = iota((GROUP, LANES), 0)
    blocks = ny // GROUP // BLOCK
    for b in range(blocks):

        def rows(g):
            return pl.ds((b * BLOCK + g) * GROUP, GROUP)

        z_flux = []
        for g in range(BLOCK):
            own, other = z[rows(g)], z_in[rows(g)]
            z_flux.append(pltpu.roll(own + other, LANES - nx, 1) * (other - own))

        def source(i, g):
            s = s_ref[i, rows(g)]
            s = jnp.where(inner, s + jnp.broadcast_to(z_flux[g][:, i : i + 1], s.shape), s)
            if b == 0 and g == 0:
                s = jnp.where(row == 0, s + bottom[i : i + 1, :], s)
            if b == blocks - 1 and g == BLOCK - 1:
                s = jnp.where(row == GROUP - 1, s + top[i : i + 1, :], s)
            return s

        first = [source(0, g) for g in range(BLOCK)]
        value = [source(1, g) for g in range(BLOCK)]
        for i in range(1, nx - 1):
            for g in range(BLOCK):
                q_ref[i, rows(g)] = r_ref[i, rows(g)] * value[g]
                first[g] = first[g] + e_ref[i, rows(g)] * value[g]
                value[g] = source(i + 1, g) + t_ref[i, rows(g)] * value[g]
        for g in range(BLOCK):
            at_group = b * BLOCK + g
            first_ground, mutual, ground, first_half, last_half = (net_ref[at_group, n] for n in range(5))
            before = left[rows(g)]
            face = first_half + jnp.where(starts, 0.0, before)
            r = reciprocal(first_ground + (mutual + face))
            t = face * r
            e = mutual * r
            first_ref[at_group, 0] = r * first[g]
            first_ref[at_group, 1] = t
            first_ref[at_group, 2] = e
            joint = mutual * t
            ground = ground + e * first_ground
            ground = jnp.where(starts, ground + joint, ground)
            ground = jnp.where(ends, ground + last_half, ground)
            send_ref[at_group, 0] = t * first_ground
            send_ref[at_group, 1] = joint
            send_ref[at_group, 2] = ground
            send_ref[at_group, 3] = t * first[g]
            send_ref[at_group, 4] = value[g] + e * first[g]


def reduced_kernel(parts, got, out):
    half = parts // 2
    ground, value = got[0, 2], got[0, 4]
    left = []
    for p in range(1, half):
        ground, value = ground + got[p, 0], value + got[p, 3]
        m = got[p, 1]
        r = reciprocal(ground + m)
        t = m * r
        left.append((value * r, t))
        ground, value = got[p, 2] + t * ground, got[p, 4] + t * value
    right = []
    ground_r, value_r = got[parts - 1, 2], got[parts - 1, 4]
    for p in range(parts - 1, half - 1, -1):
        m = got[p, 1]
        r = reciprocal(ground_r + m)
        t = m * r
        right.append((value_r * r, t))
        ground_r, value_r = got[p, 0] + t * ground_r, got[p, 3] + t * value_r
        if p > half:
            ground_r, value_r = ground_r + got[p - 1, 2], value_r + got[p - 1, 4]
    middle = (value + value_r) * reciprocal(ground + ground_r)
    cell = middle
    for p in range(half - 1, -1, -1):
        out[p, 1] = cell
        if p:
            base, slope = left[p - 1]
            cell = base + slope * cell
            out[p, 0] = cell
        else:
            out[p, 0] = jnp.zeros_like(cell)
    cell = middle
    for p in range(half, parts):
        base, slope = right[parts - 1 - p]
        out[p, 0] = cell
        cell = base + slope * cell
        out[p, 1] = cell


def back_kernel(nx, ny, ends, first, q_ref, t_ref, e_ref, out_hbm, out, sems):
    block = 4
    count = ny // GROUP // block
    copies = []
    for b in range(count):

        def rows(g):
            return pl.ds((b * block + g) * GROUP, GROUP)

        value = [ends[b * block + g, 1] for g in range(block)]
        head = []
        for g in range(block):
            at = b * block + g
            head.append(first[at, 0] + first[at, 1] * ends[at, 0] + first[at, 2] * value[g])
        for g in range(block):
            out[0, rows(g)] = head[g]
            out[nx - 1, rows(g)] = value[g]
        for i in range(nx - 2, 0, -1):
            for g in range(block):
                known = q_ref[i, rows(g)] + e_ref[i, rows(g)] * head[g]
                value[g] = known + t_ref[i, rows(g)] * value[g]
                out[i, rows(g)] = value[g]
        part = pl.ds(b * block * GROUP, block * GROUP)
        copy = pltpu.make_async_copy(out.at[:, part], out_hbm.at[:, part], sems.at[b])
        copy.start()
        copies.append(copy)
    for copy in copies:
        copy.wait()


def near(x):
    return pltpu.with_memory_space_constraint(x, pltpu.VMEM)


def far(x):
    return pltpu.with_memory_space_constraint(x, pltpu.HBM)


def call(kernel, name, outs, in_specs, out_specs, scratch=(), cost=(0, 0)):
    return pl.pallas_call(
        kernel,
        name=name,
        out_shape=outs,
        in_specs=in_specs,
        out_specs=out_specs,
        scratch_shapes=list(scratch),
        compiler_params=pltpu.CompilerParams(vmem_limit_bytes=VMEM_LIMIT),
        cost_estimate=pl.CostEstimate(flops=cost[0], bytes_accessed=cost[1], transcendentals=0),
    )


def per_device(u, kinds, axial, cross):
    nx, ny, nz = u.shape
    parts = lax.axis_size("gx")
    rows_of_y = lax.axis_size("gy")
    groups = ny // GROUP
    cells = nx * ny * nz
    field = pltpu.VMEM((nx, ny, nz), F32)
    y_face = pltpu.VMEM((2, nx, nz), F32)
    z_face = pltpu.VMEM((ny, LANES), F32)
    u_here, x, hy, hz, x_last, ya, yb, z = call(
        functools.partial(local_kernel, nx, ny),
        "local",
        (field,) * 4 + (z_face, y_face, y_face, z_face),
        [ANY_SPEC] * 4,
        (VMEM_SPEC,) * 8,
        [
            pltpu.VMEM((nx, ny, nz), jnp.int32),
            pltpu.SMEM(axial.shape, F32),
            pltpu.SMEM(cross.shape, F32),
            pltpu.SemaphoreType.DMA((2, CHUNKS)),
            pltpu.SemaphoreType.DMA((2,)),
        ],
        (60 * cells, 8 * cells),
    )(*map(far, (axial, cross, u, kinds)))
    left = lax.ppermute(x_last, "gx", [(i, (i + 1) % parts) for i in range(parts)])
    odd_pairs = [(i, i ^ 1) for i in range(rows_of_y)]
    even_pairs = [
        (2 * i + c, 2 * j + c if 0 <= j < rows_of_y else 2 * i + 1 - c)
        for i in range(rows_of_y)
        for j in (i + 1 if i % 2 else i - 1,)
        for c in range(2)
    ]
    ya_in = lax.ppermute(ya, "gy", odd_pairs)
    yb_in = lax.ppermute(yb, ("gy", "gz"), even_pairs)
    z_in = lax.ppermute(z, "gz", [(0, 1), (1, 0)])
    s, t, e, r, net = call(
        functools.partial(source_kernel, nx, ny),
        "source",
        (field,) * 4 + (pltpu.VMEM((groups, 5, GROUP, LANES), F32),),
        [VMEM_SPEC] * 4,
        (VMEM_SPEC,) * 5,
        cost=(80 * cells, 8 * cells),
    )(*map(near, (u_here, x, hy, hz)))
    q, first, send = call(
        functools.partial(forward_kernel, nx, ny),
        "forward",
        (field, pltpu.VMEM((groups, 3, GROUP, LANES), F32), pltpu.VMEM((groups, 5, GROUP, LANES), F32)),
        [VMEM_SPEC] * 12,
        (VMEM_SPEC,) * 3,
        [pltpu.VMEM((nx, nz), F32), pltpu.VMEM((nx, nz), F32)],
        (10 * cells, 8 * cells),
    )(*map(near, (left, ya, yb, z, ya_in, yb_in, z_in, s, t, e, r, net)))
    got = lax.all_to_all(send, "gx", 0, 0, tiled=True)
    solved = call(
        functools.partial(reduced_kernel, parts),
        "reduced",
        pltpu.VMEM((parts, 2, GROUP, LANES), F32),
        [VMEM_SPEC],
        VMEM_SPEC,
    )(near(got))
    ends = lax.all_to_all(solved, "gx", 0, 0, tiled=True)
    return call(
        functools.partial(back_kernel, nx, ny),
        "back",
        jax.ShapeDtypeStruct((nx, ny, nz), F32),
        [VMEM_SPEC] * 5,
        ANY_SPEC,
        [pltpu.VMEM((nx, ny, nz), F32), pltpu.SemaphoreType.DMA((ny // GROUP // 4,))],
        (4 * cells, 8 * cells),
    )(*map(near, (ends, first, q, t, e)))


def solution(mesh):
    placed = (P("gx", "gy", "gz"), P("gx", "gy", "gz"), P(), P())
    return jax.shard_map(
        per_device, mesh=mesh, in_specs=placed, out_specs=P("gx", "gy", "gz"), check_vma=False
    )
```

```python
import functools

import jax
import jax.numpy as jnp
from jax import lax
from jax.experimental import pallas as pl
from jax.experimental.pallas import tpu as pltpu
from jax.sharding import PartitionSpec as P

F32 = jnp.float32
LANES = 128
GROUP = 8
VMEM_LIMIT = 12 * 1024 * 1024
CHUNKS = 4
BLOCK = 16
SMEM_SPEC = pl.BlockSpec(memory_space=pltpu.SMEM)
VMEM_SPEC = pl.BlockSpec(memory_space=pltpu.VMEM)
ANY_SPEC = pl.BlockSpec(memory_space=pl.ANY)


def iota(shape, axis):
    return lax.broadcasted_iota(jnp.int32, shape, axis)


def half_table(table, row, classes):
    return [(table[c] if row is None else table[row, c]) * 0.5 for c in range(classes)]


def choose(table, bits):
    level = list(table)
    for bit in bits:
        half = len(level) // 2
        level = [jnp.where(bit, high, low) for low, high in zip(level[:half], level[half:])]
    return level[0]


def pick(tables, kinds):
    bits = kinds >= 4, (kinds & 2) != 0, (kinds & 1) != 0
    return [choose(table, bits) for table in tables]


def reciprocal(x):
    r = pl.reciprocal(x, approx=True)
    return r * (2.0 - x * r)


def local_kernel(
    nx, ny, axial_hbm, cross_hbm, u_hbm, kind_hbm,
    u_ref, x_ref, hy_ref, hz_ref, ya_ref, yb_ref, z_ref,
    kind_ref, axial, cross, sems, table_sems,
):
    table_copies = [
        pltpu.make_async_copy(axial_hbm, axial, table_sems.at[0]),
        pltpu.make_async_copy(cross_hbm, cross, table_sems.at[1]),
    ]
    for copy in table_copies:
        copy.start()
    step = nx // CHUNKS
    copies = []
    for c in range(CHUNKS):
        part = pl.ds(c * step, step)
        pair = (
            pltpu.make_async_copy(kind_hbm.at[part], kind_ref.at[part], sems.at[1, c]),
            pltpu.make_async_copy(u_hbm.at[part], u_ref.at[part], sems.at[0, c]),
        )
        for copy in pair:
            copy.start()
        copies.append(pair)
    for copy in table_copies:
        copy.wait()
    classes = axial.shape[0]
    kx = half_table(axial, None, classes)
    ky = half_table(cross, 0, classes)
    kz = half_table(cross, 1, classes)
    even = lax.axis_index("gy") % 2 == 0
    inner = jnp.where(lax.axis_index("gz") == 0, LANES - 1, 0)
    lane = iota((GROUP, LANES), 1)
    groups = ny // GROUP
    for i in range(nx):
        if i % step == 0:
            for copy in copies[i // step]:
                copy.wait()
        shift = lax.rem(LANES + i - inner, LANES)
        shift_k = lax.rem(LANES + nx + i - inner, LANES)
        for g in range(groups):
            rows = pl.ds(g * GROUP, GROUP)
            hx, hy, hz = pick((kx, ky, kz), kind_ref[i, rows])
            x_ref[i, rows] = hx
            hy_ref[i, rows] = hy
            hz_ref[i, rows] = hz
            packed = z_ref[rows] if i else jnp.zeros((GROUP, LANES), F32)
            packed = jnp.where(lane == i, pltpu.roll(u_ref[i, rows], shift, 1), packed)
            z_ref[rows] = jnp.where(lane == nx + i, pltpu.roll(hz, shift_k, 1), packed)
    ya_ref[0] = jnp.where(even, u_ref[:, ny - 1, :], u_ref[:, 0, :])
    ya_ref[1] = jnp.where(even, hy_ref[:, ny - 1, :], hy_ref[:, 0, :])
    yb_ref[0] = jnp.where(even, u_ref[:, 0, :], u_ref[:, ny - 1, :])
    yb_ref[1] = jnp.where(even, hy_ref[:, 0, :], hy_ref[:, ny - 1, :])


def source_kernel(nx, ny, u_ref, x_ref, hy_ref, hz_ref, s_ref, t_ref, e_ref, r_ref, net_ref):
    one = jnp.ones((GROUP, LANES), F32)
    state = [None] * (ny // GROUP)
    lane = iota((GROUP, LANES), 1)
    row = iota((GROUP, LANES), 0)
    outer = lane == jnp.where(lax.axis_index("gz") == 0, 0, LANES - 1)
    groups = ny // GROUP

    def fetch(i, g):
        rows = pl.ds(g * GROUP, GROUP)
        u, hy = u_ref[i, rows], hy_ref[i, rows]
        return u, hy, pltpu.roll(u, GROUP - 1, 0), pltpu.roll(hy, GROUP - 1, 0)

    for i in range(nx):
        now = fetch(i, 0)
        below = jnp.zeros((GROUP, LANES), F32)
        for g in range(groups):
            rows = pl.ds(g * GROUP, GROUP)
            u, hy, u_rolled, hy_rolled = now
            hz = hz_ref[i, rows]
            if g < groups - 1:
                now = fetch(i, g + 1)
                u_up = jnp.where(row == GROUP - 1, now[2], u_rolled)
                hy_up = jnp.where(row == GROUP - 1, now[3], hy_rolled)
                flux = (hy + hy_up) * (u_up - u)
            else:
                flux = jnp.where(row == GROUP - 1, 0.0, (hy + hy_rolled) * (u_rolled - u))
            down = pltpu.roll(flux, 1, 0)
            total = u + flux - jnp.where(row == 0, below, down)
            below = down
            z_up = (hz + pltpu.roll(hz, LANES - 1, 1)) * (pltpu.roll(u, LANES - 1, 1) - u)
            z_down = (hz + pltpu.roll(hz, 1, 1)) * (u - pltpu.roll(u, 1, 1))
            total = total + (jnp.where(lane == LANES - 1, 0.0, z_up) - jnp.where(lane == 0, 0.0, z_down))
            s_ref[i, rows] = jnp.where(outer, total - hz * u, total)
            after = x_ref[i, rows]
            if i == 0:
                net_ref[g, 3] = after
                state[g] = after
            elif i == 1:
                state[g] = (one, state[g] + after, one, after)
            else:
                first_ground, mutual, ground, here = state[g]
                face = here + after
                r = reciprocal(ground + (mutual + face))
                t = face * r
                e = mutual * r
                t_ref[i - 1, rows] = t
                e_ref[i - 1, rows] = e
                r_ref[i - 1, rows] = r
                state[g] = (first_ground + e * ground, mutual * t, 1.0 + t * ground, after)
    for g in range(groups):
        for n, item in zip((0, 1, 2, 4), state[g]):
            net_ref[g, n] = item


def forward_kernel(
    nx, ny, ya, yb, z, ya_in, yb_in, z_in, s_ref, t_ref, e_ref, r_ref, net_ref, q_ref, send_ref, top, bottom
):
    at, last = lax.axis_index("gy"), lax.axis_size("gy") - 1
    even = at % 2 == 0
    core = lax.axis_index("gz")

    def edge(own, other, inside):
        keep = jnp.where(inside, 1.0, 0.0)
        return (own[1] + other[1] * keep) * (other[0] * keep - own[0])

    has_up, has_down = at < last, at > 0
    flux_a = edge(ya, ya_in, jnp.where(even, has_up, has_down))
    flux_b = edge(yb, yb_in, jnp.where(even, has_down, has_up))
    top[...] = jnp.where(even, flux_a, flux_b)
    bottom[...] = jnp.where(even, flux_b, flux_a)
    inner = iota((GROUP, LANES), 1) == jnp.where(core == 0, LANES - 1, 0)
    row = iota((GROUP, LANES), 0)
    blocks = ny // GROUP // BLOCK
    for b in range(blocks):

        def rows(g):
            return pl.ds((b * BLOCK + g) * GROUP, GROUP)

        z_flux = []
        for g in range(BLOCK):
            own, other = z[rows(g)], z_in[rows(g)]
            z_flux.append(pltpu.roll(own + other, LANES - nx, 1) * (other - own))

        def source(i, g):
            s = s_ref[i, rows(g)]
            s = jnp.where(inner, s + jnp.broadcast_to(z_flux[g][:, i : i + 1], s.shape), s)
            if b == 0 and g == 0:
                s = jnp.where(row == 0, s + bottom[i : i + 1, :], s)
            if b == blocks - 1 and g == BLOCK - 1:
                s = jnp.where(row == GROUP - 1, s + top[i : i + 1, :], s)
            return s

        first = [source(0, g) for g in range(BLOCK)]
        value = [source(1, g) for g in range(BLOCK)]
        for i in range(1, nx - 1):
            for g in range(BLOCK):
                q_ref[i, rows(g)] = r_ref[i, rows(g)] * value[g]
                first[g] = first[g] + e_ref[i, rows(g)] * value[g]
                value[g] = source(i + 1, g) + t_ref[i, rows(g)] * value[g]
        for g in range(BLOCK):
            for n in range(5):
                send_ref[b * BLOCK + g, n] = net_ref[b * BLOCK + g, n]
            send_ref[b * BLOCK + g, 5] = first[g]
            send_ref[b * BLOCK + g, 6] = value[g]


def reduced_kernel(parts, got, out):
    half = parts // 2

    def inward(order, head):
        ends = (0, 2, 3, 4, 5, 6) if head else (2, 0, 4, 3, 6, 5)
        near, far, near_k, far_k, near_y, far_y = ends
        state = None
        steps = []
        for p in order:
            ground, value = got[p, near], got[p, near_y]
            joint = None
            if state is None:
                ground = ground + got[p, near_k]
            else:
                g, y, k = state
                face = k + got[p, near_k]
                r = reciprocal(g + face)
                t = face * r
                joint = (y * r, t)
                ground, value = ground + t * g, value + t * y
            m = got[p, 1]
            r = reciprocal(ground + m)
            t = m * r
            steps.append((p, joint, (value * r, t)))
            state = (got[p, far] + t * ground, got[p, far_y] + t * value, got[p, far_k])
        return state, steps

    left, left_steps = inward(range(half), True)
    right, right_steps = inward(range(parts - 1, half - 1, -1), False)
    face = left[2] + right[2]
    r = reciprocal(left[0] + face)
    t = face * r
    right_end = (right[1] + t * left[1]) * reciprocal(right[0] + t * left[0])
    left_end = left[1] * r + t * right_end

    def outward(steps, value, near, far):
        for p, joint, (base, slope) in reversed(steps):
            out[p, far] = value
            value = base + slope * value
            out[p, near] = value
            if joint is not None:
                value = joint[0] + joint[1] * value

    outward(left_steps, left_end, 0, 1)
    outward(right_steps, right_end, 1, 0)


def back_kernel(nx, ny, ends, q_ref, t_ref, e_ref, out_hbm, out, sems):
    block = 4
    count = ny // GROUP // block
    copies = []
    for b in range(count):

        def rows(g):
            return pl.ds((b * block + g) * GROUP, GROUP)

        head = [ends[b * block + g, 0] for g in range(block)]
        value = [ends[b * block + g, 1] for g in range(block)]
        for g in range(block):
            out[0, rows(g)] = head[g]
            out[nx - 1, rows(g)] = value[g]
        for i in range(nx - 2, 0, -1):
            for g in range(block):
                known = q_ref[i, rows(g)] + e_ref[i, rows(g)] * head[g]
                value[g] = known + t_ref[i, rows(g)] * value[g]
                out[i, rows(g)] = value[g]
        part = pl.ds(b * block * GROUP, block * GROUP)
        copy = pltpu.make_async_copy(out.at[:, part], out_hbm.at[:, part], sems.at[b])
        copy.start()
        copies.append(copy)
    for copy in copies:
        copy.wait()


def near(x):
    return pltpu.with_memory_space_constraint(x, pltpu.VMEM)


def far(x):
    return pltpu.with_memory_space_constraint(x, pltpu.HBM)


def call(kernel, name, outs, in_specs, out_specs, scratch=(), cost=(0, 0)):
    return pl.pallas_call(
        kernel,
        name=name,
        out_shape=outs,
        in_specs=in_specs,
        out_specs=out_specs,
        scratch_shapes=list(scratch),
        compiler_params=pltpu.CompilerParams(vmem_limit_bytes=VMEM_LIMIT),
        cost_estimate=pl.CostEstimate(flops=cost[0], bytes_accessed=cost[1], transcendentals=0),
    )


def per_device(u, kinds, axial, cross):
    nx, ny, nz = u.shape
    parts = lax.axis_size("gx")
    rows_of_y = lax.axis_size("gy")
    groups = ny // GROUP
    cells = nx * ny * nz
    field = pltpu.VMEM((nx, ny, nz), F32)
    y_face = pltpu.VMEM((2, nx, nz), F32)
    z_face = pltpu.VMEM((ny, LANES), F32)
    u_here, x, hy, hz, ya, yb, z = call(
        functools.partial(local_kernel, nx, ny),
        "local",
        (field,) * 4 + (y_face, y_face, z_face),
        [ANY_SPEC] * 4,
        (VMEM_SPEC,) * 7,
        [
            pltpu.VMEM((nx, ny, nz), jnp.int32),
            pltpu.SMEM(axial.shape, F32),
            pltpu.SMEM(cross.shape, F32),
            pltpu.SemaphoreType.DMA((2, CHUNKS)),
            pltpu.SemaphoreType.DMA((2,)),
        ],
        (60 * cells, 8 * cells),
    )(*map(far, (axial, cross, u, kinds)))
    odd_pairs = [(i, i ^ 1) for i in range(rows_of_y)]
    even_pairs = [
        (2 * i + c, 2 * j + c if 0 <= j < rows_of_y else 2 * i + 1 - c)
        for i in range(rows_of_y)
        for j in (i + 1 if i % 2 else i - 1,)
        for c in range(2)
    ]
    ya_in = lax.ppermute(ya, "gy", odd_pairs)
    yb_in = lax.ppermute(yb, ("gy", "gz"), even_pairs)
    z_in = lax.ppermute(z, "gz", [(0, 1), (1, 0)])
    s, t, e, r, net = call(
        functools.partial(source_kernel, nx, ny),
        "source",
        (field,) * 4 + (pltpu.VMEM((groups, 5, GROUP, LANES), F32),),
        [VMEM_SPEC] * 4,
        (VMEM_SPEC,) * 5,
        cost=(80 * cells, 8 * cells),
    )(*map(near, (u_here, x, hy, hz)))
    q, send = call(
        functools.partial(forward_kernel, nx, ny),
        "forward",
        (field, pltpu.VMEM((groups, 7, GROUP, LANES), F32)),
        [VMEM_SPEC] * 11,
        (VMEM_SPEC,) * 2,
        [pltpu.VMEM((nx, nz), F32), pltpu.VMEM((nx, nz), F32)],
        (10 * cells, 8 * cells),
    )(*map(near, (ya, yb, z, ya_in, yb_in, z_in, s, t, e, r, net)))
    got = lax.all_to_all(send, "gx", 0, 0, tiled=True)
    solved = call(
        functools.partial(reduced_kernel, parts),
        "reduced",
        pltpu.VMEM((parts, 2, GROUP, LANES), F32),
        [VMEM_SPEC],
        VMEM_SPEC,
    )(near(got))
    ends = lax.all_to_all(solved, "gx", 0, 0, tiled=True)
    return call(
        functools.partial(back_kernel, nx, ny),
        "back",
        jax.ShapeDtypeStruct((nx, ny, nz), F32),
        [VMEM_SPEC] * 4,
        ANY_SPEC,
        [pltpu.VMEM((nx, ny, nz), F32), pltpu.SemaphoreType.DMA((ny // GROUP // 4,))],
        (4 * cells, 8 * cells),
    )(*map(near, (ends, q, t, e)))


def solution(mesh):
    placed = (P("gx", "gy", "gz"), P("gx", "gy", "gz"), P(), P())
    return jax.shard_map(
        per_device, mesh=mesh, in_specs=placed, out_specs=P("gx", "gy", "gz"), check_vma=False
    )
```
